128 devices in a mesh: tile: 32 (over z, y, core), slab: 4 (over x).
Axes of the slice: x: 4, y: 4, z: 4, core: 2. Of those that a mesh axis runs over, the one named last changes fastest.
Arguments:
- snapshots: float32 [64, 245760], P('tile', 'slab'), as said below
- old_basis: float32 [245760, 512], P(('slab', 'tile'))
- sing_values: float32 [512], replicated, may hold values from 2 to 8
Outputs:
- new_basis: bfloat16 [245760, 512], P(('slab', 'tile'))
The draws below stay inside these ranges and needn't reach their ends.
Inputs may be any that keep to these rules, and one draw needn't show every extreme that they name: Each snapshot is a combination of the resident modes plus a residual part whose size differs strongly between snapshots and grows along the cells.
All inputs are finite; a program needn't handle non-finite values.
Results may differ from the reference program's by a relative error of at most 0.001.
Values sent between devices are 32-bit elements; how exact they have to be, the bound alone decides.
A program may use at most 64 MiB of HBM per device.

```python
import math
import jax
import jax.numpy as jnp
from jax import lax

MODES = 512
SNAPS = 64
CELLS = 245760


def common_basis(key):
    return jax.random.normal(jax.random.fold_in(key, 11), (CELLS, MODES), jnp.float32)


def draw_old_basis(key, part):
    return common_basis(key)


def draw_snapshots(key, part):
    modes_part = common_basis(key)
    mixing = 0.8 * jax.random.normal(jax.random.fold_in(key, 12), (MODES, SNAPS), jnp.float32)
    log_scale = jax.random.uniform(jax.random.fold_in(key, 13), (SNAPS,), jnp.float32, 0.0, jnp.log(10.0))
    position = jnp.arange(CELLS, dtype=jnp.float32) / CELLS
    ramp = 1.0 + 2.0 * position
    noise = jax.random.normal(jax.random.fold_in(key, 14), (SNAPS, CELLS), jnp.float32)
    signal = jnp.dot(mixing.T, modes_part.T, preferred_element_type=jnp.float32)
    return signal + noise * jnp.exp(log_scale)[:, None] * ramp[None, :]


def setup_inputs(seed: int = 0) -> dict:
    splits = jax.random.split(jax.random.key(seed), 4)
    snapshots = draw_snapshots(jax.random.fold_in(splits[3], 71), 0)
    old_basis = draw_old_basis(jax.random.fold_in(splits[3], 71), 0)
    sing_values = jnp.clip(jnp.exp(jax.random.uniform(splits[2], (MODES,), jnp.float32, math.log(2.0), math.log(8.0))), 2.0, 8.0)
    return {"snapshots": snapshots, "old_basis": old_basis, "sing_values": sing_values}


HIGH = lax.Precision.HIGHEST

def tri_solve(lower, rows):
    return lax.linalg.triangular_solve(lower, rows, left_side=True, lower=True)

def chol_rows(rows, factor):
    gram_mat = jnp.dot(rows.astype(jnp.float32), rows.T.astype(jnp.float32), precision=HIGH, preferred_element_type=jnp.float32) * factor
    lower = jnp.linalg.cholesky(gram_mat)
    return (tri_solve(lower, rows), lower)

def rotation_of(coeffs, factor_mat, sing_values):
    upper_block = jnp.diag(sing_values * sing_values) + jnp.dot(coeffs.T.astype(jnp.float32), coeffs.astype(jnp.float32), precision=HIGH, preferred_element_type=jnp.float32)
    lower_block = jnp.dot(factor_mat.T.astype(jnp.float32), coeffs.astype(jnp.float32), precision=HIGH, preferred_element_type=jnp.float32)
    stacked = jnp.concatenate([upper_block, lower_block], axis=0)
    for repeat_index in range(2):
        gram_mat = jnp.dot(stacked.T.astype(jnp.float32), stacked.astype(jnp.float32), precision=HIGH, preferred_element_type=jnp.float32)
        lower = jnp.linalg.cholesky(gram_mat)
        stacked = tri_solve(lower, stacked.T).T
    return stacked

def reference(snapshots, old_basis, sing_values):
    weight_cell = 1.0 / CELLS
    coeffs = jnp.dot(snapshots.astype(jnp.float32), old_basis.astype(jnp.float32), precision=HIGH, preferred_element_type=jnp.float32) * weight_cell
    resid = snapshots - jnp.dot(coeffs.astype(jnp.float32), old_basis.T.astype(jnp.float32), precision=HIGH, preferred_element_type=jnp.float32)
    ortho, lower_one = chol_rows(resid, weight_cell)
    rotation = rotation_of(coeffs, lower_one, sing_values)
    modes = old_basis.shape[1]
    result = jnp.dot(old_basis.astype(jnp.float32), rotation[:modes].astype(jnp.float32), precision=HIGH, preferred_element_type=jnp.float32)
    result = result + jnp.dot(ortho.T.astype(jnp.float32), rotation[modes:].astype(jnp.float32), precision=HIGH, preferred_element_type=jnp.float32)
    return result.astype(jnp.bfloat16)
```

```python
import functools

import jax
import jax.numpy as jnp
from jax import lax
from jax.experimental import pallas as pl
from jax.experimental.pallas import tpu as pltpu
from jax.sharding import PartitionSpec as P

F32, BF16 = jnp.float32, jnp.bfloat16
HIGH = lax.Precision.HIGHEST
BLK = 64


def dot6(a, b, ca=1, cb=0):
    return lax.dot_general(a, b, (((ca,), (cb,)), ((), ())), precision=HIGH, preferred_element_type=F32)


def split(a):
    hi = a.astype(BF16)
    return hi, (a - hi.astype(F32)).astype(BF16)


def dot1(a, b, ca=1, cb=0):
    return lax.dot_general(a, b, (((ca,), (cb,)), ((), ())), preferred_element_type=F32)


def dot3(a, b, ca=1, cb=0):
    (ah, al), (bh, bl) = split(a), split(b)
    return dot1(ah, bh, ca, cb) + (dot1(ah, bl, ca, cb) + dot1(al, bh, ca, cb))


def inverse_factors(mats):
    n = mats[0].shape[0]
    eye = (lax.broadcasted_iota(jnp.int32, (n, n), 0) == lax.broadcasted_iota(jnp.int32, (n, n), 1)).astype(F32)
    sub = lax.broadcasted_iota(jnp.int32, (8, 2 * n), 0)
    work = []
    for a in mats:
        both = jnp.concatenate([eye, a], axis=1)
        work.append([both[8 * r : 8 * r + 8] for r in range(n // 8)])
    scale = [[None] * (n // 8) for _ in mats]
    for j in range(n):
        r, s = divmod(j, 8)
        for m, rows in enumerate(work):
            row = jnp.broadcast_to(rows[r][s : s + 1, :], (8, 2 * n))
            pivot = jnp.broadcast_to(row[:, n + j : n + j + 1], (8, 2 * n))
            part = row * (1.0 / pivot)
            root = lax.rsqrt(pivot)
            scale[m][r] = root if s == 0 else jnp.where(sub == s, root, scale[m][r])
            for q in range(r, n // 8):
                col = jnp.broadcast_to(rows[q][:, n + j : n + j + 1], (8, 2 * n))
                if q == r:
                    col = jnp.where(sub > s, col, 0.0)
                rows[q] = rows[q] - col * part
    return [
        jnp.concatenate([rows[r] * scale[m][r] for r in range(n // 8)], axis=0)[:, :n]
        for m, rows in enumerate(work)
    ]


def weights_of(c, k_res, sing, second=True):
    snaps, modes = c.shape
    blocks = modes // BLK
    q = c / (sing * sing)
    lane = lax.broadcasted_iota(jnp.int32, (snaps, 128), 1)
    cp, cq, qq, cb, qb = [], [], [], [], []
    for k in range(blocks):
        at = (k // 2) * 128
        c2, q2 = c[:, at : at + 128], q[:, at : at + 128]
        mine = (lane // BLK) == (k % 2)
        cm, qm = jnp.where(mine, c2, 0.0), jnp.where(mine, q2, 0.0)
        cp.append(dot6(cm, c2, 1, 1))
        cq.append(dot6(cm, q2, 1, 1))
        qq.append(dot6(qm, q2, 1, 1))
        cb.append(c[:, k * BLK : (k + 1) * BLK])
        qb.append(q[:, k * BLK : (k + 1) * BLK])
    eye = (lax.broadcasted_iota(jnp.int32, (BLK, BLK), 0) == lax.broadcasted_iota(jnp.int32, (BLK, BLK), 1)).astype(F32)
    a, b, g = [None] * blocks, [None] * blocks, [None] * blocks
    run = k_res
    for k in reversed(range(blocks)):
        run = run + cp[k]
        a[k] = run
    runb, rung = eye, None
    for k in range(1, blocks):
        runb = runb + cq[k - 1]
        rung = qq[0] if k == 1 else rung + qq[k - 1]
        b[k], g[k] = runb, rung
    la = [None] + inverse_factors(a[1:])
    u = [None] + [dot6(la[k], b[k]) for k in range(1, blocks)]
    t = [None] + [dot6(la[k], cb[k]) for k in range(1, blocks)]
    lg = [None] + inverse_factors([g[k] + dot6(u[k], u[k], 0, 0) for k in range(1, blocks)])
    r = [None] + [dot6(lg[k], qb[k] + dot6(u[k], t[k], 0, 0)) for k in range(1, blocks)]
    s0 = eye + dot6(cb[0], qb[0], 0, 0) + dot6(qb[0], cb[0], 0, 0) + dot6(qb[0], dot6(a[0], qb[0]), 0, 0)
    ls = inverse_factors([s0] + [eye - dot6(t[k], t[k], 0, 0) + dot6(r[k], r[k], 0, 0) for k in range(1, blocks)])
    top, bot = [jnp.zeros((snaps, BLK), F32)], [jnp.zeros((snaps, BLK), F32)]
    for k in range(1, blocks):
        gk = dot6(lg[k], r[k], 0, 0)
        hk = dot6(la[k], dot6(u[k], gk) - t[k], 0, 0)
        top.append(dot6(hk, ls[k], 1, 1))
        bot.append(dot6(gk, ls[k], 1, 1))
    z = jnp.concatenate([jnp.concatenate(top, axis=1), jnp.concatenate(bot, axis=1)], axis=0)
    y = jnp.concatenate([c, q], axis=0)
    over = dot6(y, z, 0, 0)
    ri = lax.broadcasted_iota(jnp.int32, (modes, modes), 0) // BLK
    ci = lax.broadcasted_iota(jnp.int32, (modes, modes), 1) // BLK
    zero = jnp.zeros((BLK, BLK), F32)
    diag = jnp.concatenate(
        [jnp.concatenate([ls[k].T if j == k else zero for j in range(blocks)], axis=1) for k in range(blocks)], axis=0
    )
    w = diag - jnp.where(ri < ci, over, 0.0)
    v = dot6(q, w)
    if second:
        w, v = second_pass(c, k_res, w, v)
    return w, v


def second_pass(c, k_res, w, v):
    modes = c.shape[1]
    rot = w + dot3(c, v, 0, 0)
    gram = dot3(rot, rot, 0, 0) + dot3(v, dot3(k_res, v), 0, 0)
    ri = lax.broadcasted_iota(jnp.int32, (modes, modes), 0)
    ci = lax.broadcasted_iota(jnp.int32, (modes, modes), 1)
    half = jnp.where(ri < ci, gram, jnp.where(ri == ci, 0.5 * (gram - 1.0), 0.0)).astype(BF16)
    return w - dot1(w.astype(BF16), half), v - dot1(v.astype(BF16), half)


def update_kernel(c_ref, k_ref, s_ref, x_ref, u_ref, o_ref, wh_ref, wl_ref, vs_ref):
    @pl.when(pl.program_id(0) == 0)
    def _():
        w, v = weights_of(c_ref[...], k_ref[...], s_ref[...])
        wh, wl = split(w)
        wh_ref[...] = wh
        wl_ref[...] = wl
        vh, vl = split(v)
        vs_ref[...] = jnp.concatenate([vh, vl, vh], axis=0)

    uh, ul = split(u_ref[...])
    xh, xl = split(x_ref[...].T)
    xs = jnp.concatenate([xh, xh, xl], axis=1)
    wh = wh_ref[...]
    out = dot1(uh, wh) + dot1(uh, wl_ref[...]) + dot1(ul, wh) + dot1(xs, vs_ref[...])
    o_ref[...] = out.astype(BF16)


def update(c, k_res, sing, x, u, rows=384):
    cells, modes = u.shape
    snaps = x.shape[0]
    whole = lambda *shape: pl.BlockSpec(shape, lambda i: (0, 0))
    return pl.pallas_call(
        update_kernel,
        grid=(cells // rows,),
        out_shape=jax.ShapeDtypeStruct((cells, modes), BF16),
        in_specs=[
            whole(snaps, modes),
            whole(snaps, snaps),
            whole(1, modes),
            pl.BlockSpec((snaps, rows), lambda i: (0, i)),
            pl.BlockSpec((rows, modes), lambda i: (i, 0)),
        ],
        out_specs=pl.BlockSpec((rows, modes), lambda i: (i, 0)),
        scratch_shapes=[
            pltpu.VMEM((modes, modes), BF16),
            pltpu.VMEM((modes, modes), BF16),
            pltpu.VMEM((3 * snaps, modes), BF16),
        ],
        compiler_params=pltpu.CompilerParams(vmem_limit_bytes=48 * 2**20),
        cost_estimate=pl.CostEstimate(flops=2 * 3 * cells * modes * modes, bytes_accessed=6 * cells * modes, transcendentals=0),
    )(c, k_res, sing, x, u)


def local(snapshots, old_basis, sing_values):
    x = lax.all_to_all(snapshots, "tile", split_axis=1, concat_axis=0, tiled=True)
    cells = old_basis.shape[0] * lax.axis_size("tile") * lax.axis_size("slab")
    weight = 1.0 / cells
    c = jnp.dot(x, old_basis, precision=HIGH, preferred_element_type=F32)
    c = lax.psum(c, ("tile", "slab")) * weight
    resid = x - lax.dot_general(c, old_basis, (((1,), (1,)), ((), ())), precision=HIGH, preferred_element_type=F32)
    k_res = lax.dot_general(resid, resid, (((1,), (1,)), ((), ())), precision=HIGH, preferred_element_type=F32)
    k_res = lax.psum(k_res, ("tile", "slab")) * weight
    return update(c, k_res, sing_values[None], x, old_basis)


def solution(mesh):
    return jax.shard_map(
        local,
        mesh=mesh,
        in_specs=(P("tile", "slab"), P(("slab", "tile"), None), P()),
        out_specs=P(("slab", "tile"), None),
        check_vma=False,
    )
```

```python
import functools

import jax
import jax.numpy as jnp
from jax import lax
from jax.experimental import pallas as pl
from jax.experimental.pallas import tpu as pltpu
from jax.sharding import PartitionSpec as P

F32, BF16 = jnp.float32, jnp.bfloat16
HIGH = lax.Precision.HIGHEST
BLK = 64


def dot6(a, b, ca=1, cb=0):
    return lax.dot_general(a, b, (((ca,), (cb,)), ((), ())), precision=HIGH, preferred_element_type=F32)


def split(a):
    hi = a.astype(BF16)
    return hi, (a - hi.astype(F32)).astype(BF16)


def dot1(a, b, ca=1, cb=0):
    return lax.dot_general(a, b, (((ca,), (cb,)), ((), ())), preferred_element_type=F32)


def dot3(a, b, ca=1, cb=0):
    (ah, al), (bh, bl) = split(a), split(b)
    return dot1(ah, bh, ca, cb) + (dot1(ah, bl, ca, cb) + dot1(al, bh, ca, cb))


def inverse_factors(mats):
    n = mats[0].shape[0]
    eye = (lax.broadcasted_iota(jnp.int32, (n, n), 0) == lax.broadcasted_iota(jnp.int32, (n, n), 1)).astype(F32)
    sub = lax.broadcasted_iota(jnp.int32, (8, 2 * n), 0)
    work = []
    for a in mats:
        both = jnp.concatenate([eye, a], axis=1)
        work.append([both[8 * r : 8 * r + 8] for r in range(n // 8)])
    scale = [[None] * (n // 8) for _ in mats]
    for j in range(n):
        r, s = divmod(j, 8)
        for m, rows in enumerate(work):
            row = jnp.broadcast_to(rows[r][s : s + 1, :], (8, 2 * n))
            pivot = jnp.broadcast_to(row[:, n + j : n + j + 1], (8, 2 * n))
            part = row * (1.0 / pivot)
            root = lax.rsqrt(pivot)
            scale[m][r] = root if s == 0 else jnp.where(sub == s, root, scale[m][r])
            for q in range(r, n // 8):
                col = jnp.broadcast_to(rows[q][:, n + j : n + j + 1], (8, 2 * n))
                if q == r:
                    col = jnp.where(sub > s, col, 0.0)
                rows[q] = rows[q] - col * part
    return [
        jnp.concatenate([rows[r] * scale[m][r] for r in range(n // 8)], axis=0)[:, :n]
        for m, rows in enumerate(work)
    ]


def weights_of(c, k_res, sing, second=True):
    snaps, modes = c.shape
    blocks = modes // BLK
    q = c / (sing * sing)
    lane = lax.broadcasted_iota(jnp.int32, (snaps, 128), 1)
    cp, cq, qq, cb, qb = [], [], [], [], []
    for k in range(blocks):
        at = (k // 2) * 128
        c2, q2 = c[:, at : at + 128], q[:, at : at + 128]
        mine = (lane // BLK) == (k % 2)
        cm, qm = jnp.where(mine, c2, 0.0), jnp.where(mine, q2, 0.0)
        cp.append(dot6(cm, c2, 1, 1))
        cq.append(dot6(cm, q2, 1, 1))
        qq.append(dot6(qm, q2, 1, 1))
        cb.append(c[:, k * BLK : (k + 1) * BLK])
        qb.append(q[:, k * BLK : (k + 1) * BLK])
    eye = (lax.broadcasted_iota(jnp.int32, (BLK, BLK), 0) == lax.broadcasted_iota(jnp.int32, (BLK, BLK), 1)).astype(F32)
    a, b, g = [None] * blocks, [None] * blocks, [None] * blocks
    run = k_res
    for k in reversed(range(blocks)):
        run = run + cp[k]
        a[k] = run
    runb, rung = eye, None
    for k in range(1, blocks):
        runb = runb + cq[k - 1]
        rung = qq[0] if k == 1 else rung + qq[k - 1]
        b[k], g[k] = runb, rung
    la = [None] + inverse_factors(a[1:])
    u = [None] + [dot6(la[k], b[k]) for k in range(1, blocks)]
    t = [None] + [dot6(la[k], cb[k]) for k in range(1, blocks)]
    lg = [None] + inverse_factors([g[k] + dot6(u[k], u[k], 0, 0) for k in range(1, blocks)])
    r = [None] + [dot6(lg[k], qb[k] + dot6(u[k], t[k], 0, 0)) for k in range(1, blocks)]
    s0 = eye + dot6(cb[0], qb[0], 0, 0) + dot6(qb[0], cb[0], 0, 0) + dot6(qb[0], dot6(a[0], qb[0]), 0, 0)
    ls = inverse_factors([s0] + [eye - dot6(t[k], t[k], 0, 0) + dot6(r[k], r[k], 0, 0) for k in range(1, blocks)])
    top, bot = [jnp.zeros((snaps, BLK), F32)], [jnp.zeros((snaps, BLK), F32)]
    for k in range(1, blocks):
        gk = dot6(lg[k], r[k], 0, 0)
        hk = dot6(la[k], dot6(u[k], gk) - t[k], 0, 0)
        top.append(dot6(hk, ls[k], 1, 1))
        bot.append(dot6(gk, ls[k], 1, 1))
    z = jnp.concatenate([jnp.concatenate(top, axis=1), jnp.concatenate(bot, axis=1)], axis=0)
    y = jnp.concatenate([c, q], axis=0)
    over = dot6(y, z, 0, 0)
    ri = lax.broadcasted_iota(jnp.int32, (modes, modes), 0) // BLK
    ci = lax.broadcasted_iota(jnp.int32, (modes, modes), 1) // BLK
    zero = jnp.zeros((BLK, BLK), F32)
    diag = jnp.concatenate(
        [jnp.concatenate([ls[k].T if j == k else zero for j in range(blocks)], axis=1) for k in range(blocks)], axis=0
    )
    w = diag - jnp.where(ri < ci, over, 0.0)
    v = dot6(q, w)
    if second:
        w, v = second_pass(c, k_res, w, v)
    return w, v


def second_pass(c, k_res, w, v):
    modes = c.shape[1]
    rot = w + dot3(c, v, 0, 0)
    gram = dot3(rot, rot, 0, 0) + dot3(v, dot3(k_res, v), 0, 0)
    ri = lax.broadcasted_iota(jnp.int32, (modes, modes), 0)
    ci = lax.broadcasted_iota(jnp.int32, (modes, modes), 1)
    half = jnp.where(ri < ci, gram, jnp.where(ri == ci, 0.5 * (gram - 1.0), 0.0)).astype(BF16)
    return w - dot1(w.astype(BF16), half), v - dot1(v.astype(BF16), half)


def all_reduce(part, held, shared, total, sends, arrivals, scale):
    me, slab = lax.axis_index("tile"), lax.axis_index("slab")
    core, spot = lax.rem(me, 2), me // 2
    twin = slab * 2 + core
    spots, twins = part.shape[0], shared.shape[0]
    waits = []

    def put(src, dst, base, step, slot, device):
        copy = pltpu.make_async_remote_copy(
            src_ref=src,
            dst_ref=dst,
            send_sem=sends.at[base + step],
            recv_sem=arrivals.at[base + slot],
            device_id=device,
            device_id_type=pl.DeviceIdType.MESH,
        )
        copy.start()
        waits.append(copy)

    def take(buf, base, slot):
        pltpu.make_async_remote_copy(
            src_ref=buf.at[slot],
            dst_ref=buf.at[slot],
            send_sem=sends.at[base],
            recv_sem=arrivals.at[base + slot],
            device_id=(me, slab),
            device_id_type=pl.DeviceIdType.MESH,
        ).wait_recv()

    for d in range(1, spots):
        peer = lax.rem(spot + d, spots)
        put(part.at[peer], held.at[spot], 0, d, spot, (2 * peer + core, slab))
    held[spot] = part[spot]
    for d in range(1, spots):
        take(held, 0, lax.rem(spot + d, spots))
    shared[twin] = jnp.sum(held[...], axis=0)
    for d in range(1, twins):
        peer = lax.rem(twin + d, twins)
        put(shared.at[twin], shared.at[twin], spots, d, twin, (2 * spot + lax.rem(peer, 2), peer // 2))
    for d in range(1, twins):
        take(shared, spots, lax.rem(twin + d, twins))
    total[spot] = jnp.sum(shared[...], axis=0) * scale
    for d in range(1, spots):
        peer = lax.rem(spot + d, spots)
        put(total.at[spot], total.at[spot], spots + twins, d, spot, (2 * peer + core, slab))
    for d in range(1, spots):
        take(total, spots + twins, lax.rem(spot + d, spots))
    return waits


def gather_kernel(
    scale, snap_ref, u_ref, c_ref, k_ref, x_ref,
    u_vm, uh_ref, ul_ref, got, cpart, cheld, cshared, ctotal, kpart, kheld, kshared, ktotal,
    u_sem, own_sem, x_send, x_recv, c_send, c_recv, k_send, k_recv,
):
    me, slab = lax.axis_index("tile"), lax.axis_index("slab")
    tiles = got.shape[0]
    cells = u_vm.shape[0]
    load = pltpu.make_async_copy(u_ref, u_vm, u_sem)
    load.start()
    core, spot = lax.rem(me, 2), me // 2
    twin = slab * 2 + core
    twins = cshared.shape[0]
    barrier = pltpu.get_barrier_semaphore()
    for d in range(1, tiles):
        pl.semaphore_signal(
            barrier, inc=1, device_id=(lax.rem(me + d, tiles), slab), device_id_type=pl.DeviceIdType.MESH
        )
    for d in range(1, twins):
        peer = lax.rem(twin + d, twins)
        pl.semaphore_signal(
            barrier, inc=1, device_id=(2 * spot + lax.rem(peer, 2), peer // 2), device_id_type=pl.DeviceIdType.MESH
        )
    pl.semaphore_wait(barrier, tiles + twins - 2)

    def cut(tile):
        return snap_ref.at[:, pl.ds(pl.multiple_of(tile * cells, 128), cells)]

    waits = []
    for d in range(1, tiles):
        peer = lax.rem(me + d, tiles)
        copy = pltpu.make_async_remote_copy(
            src_ref=cut(peer),
            dst_ref=got.at[me],
            send_sem=x_send.at[d],
            recv_sem=x_recv.at[me],
            device_id=(peer, slab),
            device_id_type=pl.DeviceIdType.MESH,
        )
        copy.start()
        waits.append(copy)
    own = pltpu.make_async_copy(cut(me), got.at[me], own_sem)
    own.start()
    load.wait()
    step = 192

    @pl.loop(0, cells // step)
    def _(i):
        at = pl.ds(pl.multiple_of(i * step, step), step)
        hi, lo = split(u_vm[at, :])
        uh_ref[at, :] = hi
        ul_ref[at, :] = lo

    own.wait()
    for d in range(1, tiles):
        slot = lax.rem(me + d, tiles)
        pltpu.make_async_remote_copy(
            src_ref=got.at[slot],
            dst_ref=got.at[slot],
            send_sem=x_send.at[0],
            recv_sem=x_recv.at[slot],
            device_id=(me, slab),
            device_id_type=pl.DeviceIdType.MESH,
        ).wait_recv()
    x = jnp.concatenate([got[:, 0, :], got[:, 1, :]], axis=0)
    x_ref[...] = x
    snaps = x.shape[0]
    xh, xl = split(x)
    both = dot1(jnp.concatenate([xh, xl], axis=0), uh_ref[...])
    part = both[:snaps] + both[snaps:] + dot1(xh, ul_ref[...])
    rows, cols = cpart.shape[1:]
    across = part.shape[1] // cols
    for i in range(cpart.shape[0]):
        r, l = divmod(i, across)
        cpart[i] = part[r * rows : (r + 1) * rows, l * cols : (l + 1) * cols]
    waits += all_reduce(cpart, cheld, cshared, ctotal, c_send, c_recv, scale)
    for i in range(cpart.shape[0]):
        r, l = divmod(i, across)
        c_ref[r * rows : (r + 1) * rows, l * cols : (l + 1) * cols] = ctotal[i]
    ch, cl = split(c_ref[...])
    both = dot1(jnp.concatenate([ch, cl], axis=0), uh_ref[...], 1, 1)
    resid = x_ref[...] - (both[:snaps] + both[snaps:] + dot1(ch, ul_ref[...], 1, 1))
    square = dot3(resid, resid, 1, 1)
    half = snaps // 2
    packed = jnp.concatenate([square[:half], square[half:]], axis=1)
    krows = kpart.shape[1]
    for i in range(kpart.shape[0]):
        kpart[i] = packed[i * krows : (i + 1) * krows]
    waits += all_reduce(kpart, kheld, kshared, ktotal, k_send, k_recv, scale)
    packed = jnp.concatenate([ktotal[i] for i in range(kpart.shape[0])], axis=0)
    k_ref[:half, :] = packed[:, :snaps]
    k_ref[half:, :] = packed[:, snaps:]
    for copy in waits:
        copy.wait_send()


def gather(snapshots, u, tiles, slabs, scale):
    cells, modes = u.shape
    each = snapshots.shape[0]
    snaps = each * tiles
    spots, twins = tiles // 2, 2 * slabs
    crows, ccols = 8, snaps * modes // (8 * spots)
    krows = snaps // 2 // spots
    vmem = pl.BlockSpec(memory_space=pltpu.VMEM)
    dma = lambda n: pltpu.SemaphoreType.DMA((n,))
    block = lambda n, *shape: pltpu.VMEM((n, *shape), F32)
    steps = 2 * spots + twins
    return pl.pallas_call(
        functools.partial(gather_kernel, scale),
        out_shape=(
            jax.ShapeDtypeStruct((snaps, modes), F32),
            jax.ShapeDtypeStruct((snaps, snaps), F32),
            jax.ShapeDtypeStruct((snaps, cells), F32),
        ),
        in_specs=[pl.BlockSpec(memory_space=pl.ANY)] * 2,
        out_specs=(vmem, vmem, vmem),
        scratch_shapes=[
            pltpu.VMEM((cells, modes), F32),
            pltpu.VMEM((cells, modes), BF16),
            pltpu.VMEM((cells, modes), BF16),
            block(tiles, each, cells),
            block(spots, crows, ccols),
            block(spots, crows, ccols),
            block(twins, crows, ccols),
            block(spots, crows, ccols),
            block(spots, krows, 2 * snaps),
            block(spots, krows, 2 * snaps),
            block(twins, krows, 2 * snaps),
            block(spots, krows, 2 * snaps),
            pltpu.SemaphoreType.DMA,
            pltpu.SemaphoreType.DMA,
            dma(tiles),
            dma(tiles),
            dma(steps),
            dma(steps),
            dma(steps),
            dma(steps),
        ],
        compiler_params=pltpu.CompilerParams(
            collective_id=0, has_side_effects=True, vmem_limit_bytes=40 * 2**20
        ),
        cost_estimate=pl.CostEstimate(flops=2 * 6 * snaps * cells * modes, bytes_accessed=4 * cells * modes, transcendentals=0),
    )(snapshots, u)


def update_kernel(c_ref, k_ref, s_ref, x_ref, u_ref, o_ref, wh_ref, wl_ref, vs_ref):
    @pl.when(pl.program_id(0) == 0)
    def _():
        w, v = weights_of(c_ref[...], k_ref[...], s_ref[...])
        wh, wl = split(w)
        wh_ref[...] = wh
        wl_ref[...] = wl
        vh, vl = split(v)
        vs_ref[...] = jnp.concatenate([vh, vl, vh], axis=0)

    uh, ul = split(u_ref[...])
    xh, xl = split(x_ref[...].T)
    xs = jnp.concatenate([xh, xh, xl], axis=1)
    wh = wh_ref[...]
    out = dot1(uh, wh) + dot1(uh, wl_ref[...]) + dot1(ul, wh) + dot1(xs, vs_ref[...])
    o_ref[...] = out.astype(BF16)


def update(c, k_res, sing, x, u, rows=384):
    cells, modes = u.shape
    snaps = x.shape[0]
    whole = lambda *shape: pl.BlockSpec(shape, lambda i: (0, 0))
    return pl.pallas_call(
        update_kernel,
        grid=(cells // rows,),
        out_shape=jax.ShapeDtypeStruct((cells, modes), BF16),
        in_specs=[
            whole(snaps, modes),
            whole(snaps, snaps),
            whole(1, modes),
            pl.BlockSpec((snaps, rows), lambda i: (0, i)),
            pl.BlockSpec((rows, modes), lambda i: (i, 0)),
        ],
        out_specs=pl.BlockSpec((rows, modes), lambda i: (i, 0)),
        scratch_shapes=[
            pltpu.VMEM((modes, modes), BF16),
            pltpu.VMEM((modes, modes), BF16),
            pltpu.VMEM((3 * snaps, modes), BF16),
        ],
        compiler_params=pltpu.CompilerParams(vmem_limit_bytes=48 * 2**20),
        cost_estimate=pl.CostEstimate(flops=2 * 3 * cells * modes * modes, bytes_accessed=6 * cells * modes, transcendentals=0),
    )(c, k_res, sing, x, u)


def local(snapshots, old_basis, sing_values):
    tiles, slabs = lax.axis_size("tile"), lax.axis_size("slab")
    cells = old_basis.shape[0] * tiles * slabs
    c, k_res, x = gather(snapshots, old_basis, tiles, slabs, 1.0 / cells)
    return update(c, k_res, sing_values[None], x, old_basis)


def solution(mesh):
    return jax.shard_map(
        local,
        mesh=mesh,
        in_specs=(P("tile", "slab"), P(("slab", "tile"), None), P()),
        out_specs=P(("slab", "tile"), None),
        check_vma=False,
    )
```

```python
import functools

import jax
import jax.numpy as jnp
from jax import lax
from jax.experimental import pallas as pl
from jax.experimental.pallas import tpu as pltpu
from jax.sharding import PartitionSpec as P

F32, BF16 = jnp.float32, jnp.bfloat16
HIGH = lax.Precision.HIGHEST
BLK = 64


def dot6(a, b, ca=1, cb=0):
    return lax.dot_general(a, b, (((ca,), (cb,)), ((), ())), precision=HIGH, preferred_element_type=F32)


def split(a):
    hi = a.astype(BF16)
    return hi, (a - hi.astype(F32)).astype(BF16)


def dot1(a, b, ca=1, cb=0):
    return lax.dot_general(a, b, (((ca,), (cb,)), ((), ())), preferred_element_type=F32)


def dot3(a, b, ca=1, cb=0):
    (ah, al), (bh, bl) = split(a), split(b)
    return dot1(ah, bh, ca, cb) + (dot1(ah, bl, ca, cb) + dot1(al, bh, ca, cb))


def inverse_pairs(pairs, wide=4):
    n = pairs[0].shape[0]
    full = (8, 2 * n)
    sub = lax.broadcasted_iota(jnp.int32, full, 0)
    lane = lax.broadcasted_iota(jnp.int32, full, 1)
    own, base = lane % n, (lane // n) * n
    work = [[a[8 * r : 8 * r + 8] for r in range(n // 8)] for a in pairs]
    done = [[None] * n for _ in pairs]

    def spread(v, at):
        return jnp.take_along_axis(v, base + at, axis=1)

    for j in range(0, n, wide):
        r, s = divmod(j, 8)
        first = r if s + wide < 8 else r + 1
        inside = (own >= j) & (own < j + wide)
        for m, rows in enumerate(work):
            row = [jnp.broadcast_to(rows[r][s + i : s + i + 1, :], full) for i in range(wide)]
            e = {(i, l): spread(row[i], j + l) for i in range(wide) for l in range(i, wide)}
            col = {(q, i): spread(rows[q], j + i) for q in range(first, n // 8) for i in range(wide)}
            if first == r:
                for i in range(wide):
                    col[r, i] = jnp.where(sub >= s + wide, col[r, i], 0.0)
            row = [jnp.where(inside, jnp.where(own == j + i, 1.0, 0.0), row[i]) for i in range(wide)]
            part, f = [], {}
            for i in range(wide):
                inv = 1.0 / e[i, i]
                part.append(row[i] * inv)
                done[m][j + i] = row[i] * lax.rsqrt(e[i, i])
                for l in range(i + 1, wide):
                    f[i, l] = e[i, l] * inv
                    row[l] = row[l] - f[i, l] * row[i]
                    for p in range(l, wide):
                        e[l, p] = e[l, p] - f[i, l] * e[i, p]
            for i in reversed(range(wide - 1)):
                for l in reversed(range(i + 1, wide)):
                    part[i] = part[i] - f[i, l] * part[l]
            for q in range(first, n // 8):
                fall = col[q, 0] * part[0]
                for i in range(1, wide):
                    fall = fall + col[q, i] * part[i]
                keep = inside & (sub >= s + wide) if q == r else inside
                rows[q] = jnp.where(keep, 0.0, rows[q]) - fall
    outs = []
    for m in range(len(pairs)):
        pieces = []
        for r in range(n // 8):
            piece = done[m][8 * r]
            for s in range(1, 8):
                piece = jnp.where(sub == s, done[m][8 * r + s], piece)
            pieces.append(jnp.where(own <= sub + 8 * r, piece, 0.0))
        outs.append(jnp.concatenate(pieces, axis=0))
    return outs


def inverse_factors(mats):
    n = mats[0].shape[0]
    odd = len(mats) % 2
    mats = mats + mats[:1] * odd
    pairs = [jnp.concatenate(mats[i : i + 2], axis=1) for i in range(0, len(mats), 2)]
    outs = []
    for p in inverse_pairs(pairs):
        outs += [p[:, :n], p[:, n:]]
    return outs[: len(outs) - odd]


def weights_of(c, k_res, sing, second=True):
    snaps, modes = c.shape
    blocks = modes // BLK
    q = c / (sing * sing)
    lane = lax.broadcasted_iota(jnp.int32, (snaps, 128), 1)
    cp, cq, qq, cb, qb = [], [], [], [], []
    for k in range(blocks):
        at = (k // 2) * 128
        c2, q2 = c[:, at : at + 128], q[:, at : at + 128]
        mine = (lane // BLK) == (k % 2)
        cm, qm = jnp.where(mine, c2, 0.0), jnp.where(mine, q2, 0.0)
        cp.append(dot6(cm, c2, 1, 1))
        cq.append(dot6(cm, q2, 1, 1))
        qq.append(dot6(qm, q2, 1, 1))
        cb.append(c[:, k * BLK : (k + 1) * BLK])
        qb.append(q[:, k * BLK : (k + 1) * BLK])
    eye = (lax.broadcasted_iota(jnp.int32, (BLK, BLK), 0) == lax.broadcasted_iota(jnp.int32, (BLK, BLK), 1)).astype(F32)
    a, b, g = [None] * blocks, [None] * blocks, [None] * blocks
    run = k_res
    for k in reversed(range(blocks)):
        run = run + cp[k]
        a[k] = run
    runb, rung = eye, None
    for k in range(1, blocks):
        runb = runb + cq[k - 1]
        rung = qq[0] if k == 1 else rung + qq[k - 1]
        b[k], g[k] = runb, rung
    la = [None] + inverse_factors(a[1:])
    u = [None] + [dot6(la[k], b[k]) for k in range(1, blocks)]
    t = [None] + [dot6(la[k], cb[k]) for k in range(1, blocks)]
    lg = [None] + inverse_factors([g[k] + dot6(u[k], u[k], 0, 0) for k in range(1, blocks)])
    r = [None] + [dot6(lg[k], qb[k] + dot6(u[k], t[k], 0, 0)) for k in range(1, blocks)]
    s0 = eye + dot6(cb[0], qb[0], 0, 0) + dot6(qb[0], cb[0], 0, 0) + dot6(qb[0], dot6(a[0], qb[0]), 0, 0)
    ls = inverse_factors([s0] + [eye - dot6(t[k], t[k], 0, 0) + dot6(r[k], r[k], 0, 0) for k in range(1, blocks)])
    top, bot = [jnp.zeros((snaps, BLK), F32)], [jnp.zeros((snaps, BLK), F32)]
    for k in range(1, blocks):
        gk = dot6(lg[k], r[k], 0, 0)
        hk = dot6(la[k], dot6(u[k], gk) - t[k], 0, 0)
        top.append(dot6(hk, ls[k], 1, 1))
        bot.append(dot6(gk, ls[k], 1, 1))
    z = jnp.concatenate([jnp.concatenate(top, axis=1), jnp.concatenate(bot, axis=1)], axis=0)
    y = jnp.concatenate([c, q], axis=0)
    over = dot6(y, z, 0, 0)
    ri = lax.broadcasted_iota(jnp.int32, (modes, modes), 0) // BLK
    ci = lax.broadcasted_iota(jnp.int32, (modes, modes), 1) // BLK
    zero = jnp.zeros((BLK, BLK), F32)
    diag = jnp.concatenate(
        [jnp.concatenate([ls[k].T if j == k else zero for j in range(blocks)], axis=1) for k in range(blocks)], axis=0
    )
    w = diag - jnp.where(ri < ci, over, 0.0)
    v = dot6(q, w)
    if second:
        w, v = second_pass(c, k_res, w, v)
    return w, v


def second_pass(c, k_res, w, v):
    modes = c.shape[1]
    rot = w + dot3(c, v, 0, 0)
    gram = dot3(rot, rot, 0, 0) + dot3(v, dot3(k_res, v), 0, 0)
    ri = lax.broadcasted_iota(jnp.int32, (modes, modes), 0)
    ci = lax.broadcasted_iota(jnp.int32, (modes, modes), 1)
    half = jnp.where(ri < ci, gram, jnp.where(ri == ci, 0.5 * (gram - 1.0), 0.0)).astype(BF16)
    return w - dot1(w.astype(BF16), half), v - dot1(v.astype(BF16), half)


def route(sends, arrivals):
    started = []

    def put(src, dst, step, slot, device):
        copy = pltpu.make_async_remote_copy(
            src_ref=src,
            dst_ref=dst,
            send_sem=sends.at[step],
            recv_sem=arrivals.at[slot],
            device_id=device,
            device_id_type=pl.DeviceIdType.MESH,
        )
        copy.start()
        started.append(copy)

    def take(buf, at, slot):
        pltpu.make_async_remote_copy(
            src_ref=buf.at[at],
            dst_ref=buf.at[at],
            send_sem=sends.at[0],
            recv_sem=arrivals.at[slot],
            device_id=(lax.axis_index("tile"), lax.axis_index("slab")),
            device_id_type=pl.DeviceIdType.MESH,
        ).wait_recv()

    return put, take, started


def place():
    me, slab = lax.axis_index("tile"), lax.axis_index("slab")
    core, spot = lax.rem(me, 2), me // 2
    return me, slab, core, spot, slab * 2 + core


def share(buf, base, far, put, take):
    me, slab, core, spot, twin = place()
    n, mine = buf.shape[0], spot if far else twin
    for d in range(1, n):
        peer = lax.rem(mine + d, n)
        device = (2 * peer + core, slab) if far else (2 * spot + lax.rem(peer, 2), peer // 2)
        put(buf.at[mine], buf.at[mine], base + d, base + mine, device)
    for d in range(1, n):
        slot = lax.rem(mine + d, n)
        take(buf, slot, base + slot)


def sum_by_owner(part, held, shared, total, sends, arrivals, scale):
    me, slab, core, spot, twin = place()
    spots, twins = part.shape[0], shared.shape[0]
    put, take, started = route(sends, arrivals)
    for d in range(1, spots):
        peer = lax.rem(spot + d, spots)
        put(part.at[peer], held.at[spot], d, spot, (2 * peer + core, slab))
    held[spot] = part[spot]
    for d in range(1, spots):
        slot = lax.rem(spot + d, spots)
        take(held, slot, slot)
    shared[twin] = jnp.sum(held[...], axis=0)
    share(shared, spots, False, put, take)
    total[spot] = jnp.sum(shared[...], axis=0) * scale
    share(total, spots + twins, True, put, take)
    return started


def sum_whole(part, far, near, sends, arrivals, scale):
    me, slab, core, spot, twin = place()
    put, take, started = route(sends, arrivals)
    near[twin] = part
    share(near, 0, False, put, take)
    far[spot] = jnp.sum(near[...], axis=0)
    share(far, near.shape[0], True, put, take)
    return jnp.sum(far[...], axis=0) * scale, started


def gather_kernel(
    scale, snap_ref, u_ref, c_ref, k_ref, x_ref,
    u_vm, uh_ref, ul_ref, got, cpart, cheld, cshared, ctotal, kfar, knear,
    u_sem, own_sem, x_send, x_recv, c_send, c_recv, k_send, k_recv,
):
    me, slab = lax.axis_index("tile"), lax.axis_index("slab")
    tiles = got.shape[0]
    cells = u_vm.shape[0]
    load = pltpu.make_async_copy(u_ref, u_vm, u_sem)
    load.start()
    core, spot = lax.rem(me, 2), me // 2
    twin = slab * 2 + core
    twins = cshared.shape[0]
    barrier = pltpu.get_barrier_semaphore()
    for d in range(1, tiles):
        pl.semaphore_signal(
            barrier, inc=1, device_id=(lax.rem(me + d, tiles), slab), device_id_type=pl.DeviceIdType.MESH
        )
    for d in range(1, twins):
        peer = lax.rem(twin + d, twins)
        pl.semaphore_signal(
            barrier, inc=1, device_id=(2 * spot + lax.rem(peer, 2), peer // 2), device_id_type=pl.DeviceIdType.MESH
        )
    pl.semaphore_wait(barrier, tiles + twins - 2)

    def cut(tile):
        return snap_ref.at[:, pl.ds(pl.multiple_of(tile * cells, 128), cells)]

    waits = []
    for d in range(1, tiles):
        peer = lax.rem(me + d, tiles)
        copy = pltpu.make_async_remote_copy(
            src_ref=cut(peer),
            dst_ref=got.at[me],
            send_sem=x_send.at[d],
            recv_sem=x_recv.at[me],
            device_id=(peer, slab),
            device_id_type=pl.DeviceIdType.MESH,
        )
        copy.start()
        waits.append(copy)
    own = pltpu.make_async_copy(cut(me), got.at[me], own_sem)
    own.start()
    load.wait()
    step = 192

    @pl.loop(0, cells // step)
    def _(i):
        at = pl.ds(pl.multiple_of(i * step, step), step)
        hi, lo = split(u_vm[at, :])
        uh_ref[at, :] = hi
        ul_ref[at, :] = lo

    own.wait()
    for d in range(1, tiles):
        slot = lax.rem(me + d, tiles)
        pltpu.make_async_remote_copy(
            src_ref=got.at[slot],
            dst_ref=got.at[slot],
            send_sem=x_send.at[0],
            recv_sem=x_recv.at[slot],
            device_id=(me, slab),
            device_id_type=pl.DeviceIdType.MESH,
        ).wait_recv()
    x = jnp.concatenate([got[:, 0, :], got[:, 1, :]], axis=0)
    x_ref[...] = x
    snaps = x.shape[0]
    xh, xl = split(x)
    both = dot1(jnp.concatenate([xh, xl], axis=0), uh_ref[...])
    part = both[:snaps] + both[snaps:] + dot1(xh, ul_ref[...])
    rows, cols = cpart.shape[1:]
    across = part.shape[1] // cols
    for i in range(cpart.shape[0]):
        r, l = divmod(i, across)
        cpart[i] = part[r * rows : (r + 1) * rows, l * cols : (l + 1) * cols]
    waits += sum_by_owner(cpart, cheld, cshared, ctotal, c_send, c_recv, scale)
    for i in range(cpart.shape[0]):
        r, l = divmod(i, across)
        c_ref[r * rows : (r + 1) * rows, l * cols : (l + 1) * cols] = ctotal[i]
    ch, cl = split(c_ref[...])
    both = dot1(jnp.concatenate([ch, cl], axis=0), uh_ref[...], 1, 1)
    resid = x_ref[...] - (both[:snaps] + both[snaps:] + dot1(ch, ul_ref[...], 1, 1))
    square = dot3(resid, resid, 1, 1)
    half = snaps // 2
    packed = jnp.concatenate([square[:half], square[half:]], axis=1)
    packed, more = sum_whole(packed, kfar, knear, k_send, k_recv, scale)
    waits += more
    k_ref[:half, :] = packed[:, :snaps]
    k_ref[half:, :] = packed[:, snaps:]
    for copy in waits:
        copy.wait_send()


def gather(snapshots, u, tiles, slabs, scale):
    cells, modes = u.shape
    each = snapshots.shape[0]
    snaps = each * tiles
    spots, twins = tiles // 2, 2 * slabs
    crows, ccols = 8, snaps * modes // (8 * spots)
    vmem = pl.BlockSpec(memory_space=pltpu.VMEM)
    dma = lambda n: pltpu.SemaphoreType.DMA((n,))
    block = lambda n, *shape: pltpu.VMEM((n, *shape), F32)
    steps = 2 * spots + twins
    return pl.pallas_call(
        functools.partial(gather_kernel, scale),
        out_shape=(
            jax.ShapeDtypeStruct((snaps, modes), F32),
            jax.ShapeDtypeStruct((snaps, snaps), F32),
            jax.ShapeDtypeStruct((snaps, cells), F32),
        ),
        in_specs=[pl.BlockSpec(memory_space=pl.ANY)] * 2,
        out_specs=(vmem, vmem, vmem),
        scratch_shapes=[
            pltpu.VMEM((cells, modes), F32),
            pltpu.VMEM((cells, modes), BF16),
            pltpu.VMEM((cells, modes), BF16),
            block(tiles, each, cells),
            block(spots, crows, ccols),
            block(spots, crows, ccols),
            block(twins, crows, ccols),
            block(spots, crows, ccols),
            block(spots, snaps // 2, 2 * snaps),
            block(twins, snaps // 2, 2 * snaps),
            pltpu.SemaphoreType.DMA,
            pltpu.SemaphoreType.DMA,
            dma(tiles),
            dma(tiles),
            dma(steps),
            dma(steps),
            dma(spots + twins),
            dma(spots + twins),
        ],
        compiler_params=pltpu.CompilerParams(
            collective_id=0, has_side_effects=True, vmem_limit_bytes=60 * 2**20
        ),
        cost_estimate=pl.CostEstimate(flops=2 * 6 * snaps * cells * modes, bytes_accessed=4 * cells * modes, transcendentals=0),
    )(snapshots, u)


def update_kernel(c_ref, k_ref, s_ref, x_ref, u_ref, o_ref, wh_ref, wl_ref, vs_ref):
    @pl.when(pl.program_id(0) == 0)
    def _():
        w, v = weights_of(c_ref[...], k_ref[...], s_ref[...])
        wh, wl = split(w)
        wh_ref[...] = wh
        wl_ref[...] = wl
        vh, vl = split(v)
        vs_ref[...] = jnp.concatenate([vh, vl, vh], axis=0)

    uh, ul = split(u_ref[...])
    xh, xl = split(x_ref[...].T)
    xs = jnp.concatenate([xh, xh, xl], axis=1)
    wh = wh_ref[...]
    out = dot1(uh, wh) + dot1(uh, wl_ref[...]) + dot1(ul, wh) + dot1(xs, vs_ref[...])
    o_ref[...] = out.astype(BF16)


def update(c, k_res, sing, x, u, rows=384):
    cells, modes = u.shape
    snaps = x.shape[0]
    whole = lambda *shape: pl.BlockSpec(shape, lambda i: (0, 0))
    return pl.pallas_call(
        update_kernel,
        grid=(cells // rows,),
        out_shape=jax.ShapeDtypeStruct((cells, modes), BF16),
        in_specs=[
            whole(snaps, modes),
            whole(snaps, snaps),
            whole(1, modes),
            pl.BlockSpec((snaps, rows), lambda i: (0, i)),
            pl.BlockSpec((rows, modes), lambda i: (i, 0)),
        ],
        out_specs=pl.BlockSpec((rows, modes), lambda i: (i, 0)),
        scratch_shapes=[
            pltpu.VMEM((modes, modes), BF16),
            pltpu.VMEM((modes, modes), BF16),
            pltpu.VMEM((3 * snaps, modes), BF16),
        ],
        compiler_params=pltpu.CompilerParams(vmem_limit_bytes=60 * 2**20),
        cost_estimate=pl.CostEstimate(flops=2 * 3 * cells * modes * modes, bytes_accessed=6 * cells * modes, transcendentals=0),
    )(c, k_res, sing, x, u)


def local(snapshots, old_basis, sing_values):
    tiles, slabs = lax.axis_size("tile"), lax.axis_size("slab")
    cells = old_basis.shape[0] * tiles * slabs
    c, k_res, x = gather(snapshots, old_basis, tiles, slabs, 1.0 / cells)
    return update(c, k_res, sing_values[None], x, old_basis)


def solution(mesh):
    return jax.shard_map(
        local,
        mesh=mesh,
        in_specs=(P("tile", "slab"), P(("slab", "tile"), None), P()),
        out_specs=P(("slab", "tile"), None),
        check_vma=False,
    )
```
